256 devices in a mesh: group: 8 (over z), seq: 32 (over x, y, core).
Axes of the slice: x: 4, y: 4, z: 8, core: 2. Of those that a mesh axis runs over, the one named last changes fastest.
Arguments:
- latents: bfloat16 [8, 32, 512, 1152], P(None, 'seq', 'group'), may hold values from -6 to 6
- sampler_order: int32 [8], replicated, may hold values from 0 to 7, each once
- frame_counts: int32 [8], replicated, may hold values from 16 to 32, as said below
- modulation: float32 [8, 6, 1152], replicated, may hold values from -4 to 4
- spatial_project: bfloat16 [1152, 3456], P(None, 'seq'), may hold values from -0.1875 to 0.1875
- spatial_output: bfloat16 [1152, 1152], P(None, 'seq'), may hold values from -0.1875 to 0.1875
- spatial_gain: float32 [2, 72], replicated, may hold values from 0.5 to 3
- temporal_project: bfloat16 [1152, 3456], P(None, 'seq'), may hold values from -0.1875 to 0.1875
- temporal_output: bfloat16 [1152, 1152], P(None, 'seq'), may hold values from -0.1875 to 0.1875
- temporal_gain: float32 [2, 72], replicated, may hold values from 0.5 to 3
Outputs:
- block_output: bfloat16 [8, 32, 512, 1152], P('group', 'seq')
The draws below stay inside these ranges and needn't reach their ends.
Inputs may be any that keep to these rules, and one draw needn't show every extreme that they name: `sampler_order`: a permutation of the clip ids. `frame_counts`: some clip has exactly 32 frames and some clip exactly half of 32.
All inputs are finite; a program needn't handle non-finite values.
Results may differ from the reference program's by a relative error of at most 0.022.
Values may be sent and summed in bfloat16 or wider, within the bound.
A program may use at most 128 MiB of HBM per device.

```python
import math
import jax
import jax.numpy as jnp
from jax import lax

D = 1152
HEADS = 16
HD = 72
FRAMES = 32
S = 512
CLIPS = 8


def draw_frame_counts(key, part):
    key = jax.random.fold_in(key, 11)
    first_key, second_key = jax.random.split(key)
    counts = jax.random.randint(first_key, (CLIPS,), FRAMES // 2, FRAMES + 1)
    picks = jax.random.permutation(second_key, CLIPS)
    counts = counts.at[picks[0]].set(FRAMES)
    counts = counts.at[picks[1]].set(FRAMES // 2)
    return counts.astype(jnp.int32)


def level_of(rng, shape, cuts, low, high):
    loudness = 1.0
    for axis_at, parts in cuts:
        steps = jax.random.uniform(jax.random.fold_in(jax.random.fold_in(rng, 6), axis_at), (parts,), jnp.float32, low / len(cuts), high / len(cuts))
        loudness = loudness * jnp.repeat(jnp.exp(steps), shape[axis_at] // parts).reshape((-1,) + (1,) * (len(shape) - 1 - axis_at))
    return loudness


def centred(stream_key, shape, deviation, most, cuts=(), kind=jnp.bfloat16):
    entries = jax.random.normal(stream_key, shape, jnp.float32) * deviation
    if len(cuts) > 0:
        entries = level_of(stream_key, shape, cuts, -0.22, 0.18) * entries
    return jnp.clip(entries, min=-most, max=most).astype(kind)


def setup_inputs(seed: int = 0) -> dict:
    splits = jax.random.split(jax.random.key(seed), 11)
    return {
        "latents": centred(splits[0], (CLIPS, FRAMES, S, D), 1.0, 6.0, ((1, 32), (2, 8))),
        "sampler_order": jax.random.permutation(splits[1], CLIPS).astype(jnp.int32),
        "frame_counts": draw_frame_counts(jax.random.fold_in(splits[10], 71), 0),
        "modulation": centred(splits[3], (CLIPS, 6, D), 1.0, 4.0, (), jnp.float32),
        "spatial_project": centred(splits[4], (D, 3 * D), D ** -0.5, 0.1875, ((1, 32),)),
        "spatial_output": centred(splits[5], (D, D), D ** -0.5, 0.1875, ((1, 32),)),
        "spatial_gain": jnp.clip(jax.random.uniform(splits[6], (2, HD), jnp.float32, 0.5, 3.0), 0.5, 3.0),
        "temporal_project": centred(splits[7], (D, 3 * D), D ** -0.5, 0.1875, ((1, 32),)),
        "temporal_output": centred(splits[8], (D, D), D ** -0.5, 0.1875, ((1, 32),)),
        "temporal_gain": jnp.clip(jax.random.uniform(splits[9], (2, HD), jnp.float32, 0.5, 3.0), 0.5, 3.0),
    }


EPSILON = 1e-06

def layer_norm(values):
    center = values - lax.optimization_barrier(jnp.mean(values, axis=-1, keepdims=True))
    spread = lax.optimization_barrier(jnp.mean(center * center, axis=-1, keepdims=True))
    return center * lax.rsqrt(spread + EPSILON)

def modulated(tokens, offset, stretch):
    return (layer_norm(tokens.astype(jnp.float32)) * (1.0 + stretch) + offset).astype(jnp.bfloat16)

def head_norm(values, norm_gain):
    values = values.astype(jnp.float32)
    square = lax.optimization_barrier(jnp.mean(values * values, axis=-1, keepdims=True))
    return values * lax.rsqrt(square + EPSILON) * norm_gain

def rotary(values, frame_ids):
    half_size = values.shape[-1] // 2
    frequency = jnp.power(10000.0, -2.0 * jnp.arange(half_size, dtype=jnp.float32) / values.shape[-1])
    angles = frame_ids[..., None] * frequency
    cosine = jnp.cos(angles)
    sine_part = jnp.sin(angles)
    first_half = values[..., :half_size]
    second = values[..., half_size:]
    return jnp.concatenate([first_half * cosine - second * sine_part, second * cosine + first_half * sine_part], axis=-1)

def spatial_block(tokens, project, output, norm_gain, offset, stretch, gating):
    row_count, model_width = tokens.shape
    head_size = model_width // HEADS
    hidden = modulated(tokens, offset, stretch)
    projected = jnp.dot(hidden, project, preferred_element_type=jnp.float32).astype(jnp.bfloat16)
    projected = projected.reshape(row_count, 3, HEADS, head_size)
    query_rows = head_norm(projected[:, 0], norm_gain[0]).astype(jnp.bfloat16)
    key_rows = head_norm(projected[:, 1], norm_gain[1]).astype(jnp.bfloat16)
    scores = jnp.einsum('qhd,khd->hqk', query_rows.astype(jnp.float32), key_rows.astype(jnp.float32), precision=lax.Precision.HIGHEST) / math.sqrt(head_size)
    exponent = jnp.exp(scores)
    weights = (exponent / lax.optimization_barrier(jnp.sum(exponent, axis=-1, keepdims=True))).astype(jnp.bfloat16)
    attended = jnp.einsum('hqk,khd->qhd', weights.astype(jnp.float32), projected[:, 2].astype(jnp.float32), precision=lax.Precision.HIGHEST).astype(jnp.bfloat16)
    update = jnp.dot(attended.reshape(row_count, model_width), output, preferred_element_type=jnp.float32)
    return (tokens.astype(jnp.float32) + gating * update).astype(jnp.bfloat16)

def temporal_attend(projected, norm_gain, length):
    frames, places, triple = projected.shape
    model_width = triple // 3
    head_size = model_width // HEADS
    projected = projected.reshape(frames, places, 3, HEADS, head_size)
    frame_ids = jnp.arange(frames, dtype=jnp.float32)[:, None, None]
    query_rows = rotary(head_norm(projected[:, :, 0], norm_gain[0]), frame_ids).astype(jnp.bfloat16)
    key_rows = rotary(head_norm(projected[:, :, 1], norm_gain[1]), frame_ids).astype(jnp.bfloat16)
    scores = jnp.einsum('fphd,gphd->phfg', query_rows.astype(jnp.float32), key_rows.astype(jnp.float32), precision=lax.Precision.HIGHEST) / math.sqrt(head_size)
    live_keys = jnp.arange(frames, dtype=jnp.int32) < length
    exponent = jnp.where(live_keys, jnp.exp(scores), 0.0)
    weights = (exponent / lax.optimization_barrier(jnp.sum(exponent, axis=-1, keepdims=True))).astype(jnp.bfloat16)
    attended = jnp.einsum('phfg,gphd->fphd', weights.astype(jnp.float32), projected[:, :, 2].astype(jnp.float32), precision=lax.Precision.HIGHEST)
    return attended.astype(jnp.bfloat16).reshape(frames, places, model_width)

def reference(latents, sampler_order, frame_counts, modulation, spatial_project, spatial_output, spatial_gain, temporal_project, temporal_output, temporal_gain):

    def one_group(group_id):
        clip_id = sampler_order[group_id]
        length = frame_counts[clip_id]
        modulate_rows = lax.dynamic_index_in_dim(modulation, clip_id, 0, keepdims=False)
        clip_tokens = lax.dynamic_index_in_dim(latents, clip_id, 0, keepdims=False)

        def one_frame(tokens):
            return spatial_block(tokens, spatial_project, spatial_output, spatial_gain, modulate_rows[0], modulate_rows[1], modulate_rows[2])
        mixture = lax.map(one_frame, clip_tokens)
        frames, places, model_width = mixture.shape
        hidden = modulated(mixture.reshape(frames * places, model_width), modulate_rows[3], modulate_rows[4])
        projected = jnp.dot(hidden, temporal_project, preferred_element_type=jnp.float32).astype(jnp.bfloat16)
        attended = temporal_attend(projected.reshape(frames, places, 3 * model_width), temporal_gain, length)
        update = jnp.dot(attended.reshape(frames * places, model_width), temporal_output, preferred_element_type=jnp.float32)
        update = update.reshape(frames, places, model_width)
        live_frames = (jnp.arange(frames, dtype=jnp.int32) < length).astype(jnp.float32)[:, None, None]
        return ((mixture.astype(jnp.float32) + modulate_rows[5] * update) * live_frames).astype(jnp.bfloat16)
    return lax.map(one_group, jnp.arange(CLIPS, dtype=jnp.int32))
```

```python
import functools
import math

import jax
import jax.numpy as jnp
from jax import lax
from jax.experimental import pallas as pl
from jax.experimental.pallas import tpu as pltpu
from jax.sharding import PartitionSpec as P

HEADS = 16
HD = 72
D = 1152
T = 512
SHARDS = 32
QKV_ROWS = 108
OUT_ROWS = 36
ROWS = QKV_ROWS + OUT_ROWS
EPSILON = 1e-06
SCALE = math.log2(math.e) / math.sqrt(HD)


def block_kernel(temporal, *refs):
    if temporal:
        (length_ref, tokens_ref, weights_ref, mod_ref, gain_ref, cos_ref, sin_ref,
         out_ref, hidden, qkv, attended, attended_bf, wo, update, mask) = refs
    else:
        (tokens_ref, weights_ref, mod_ref, gain_ref,
         out_ref, hidden, qkv, attended, attended_bf, wo, update) = refs

    offset, stretch, gating = mod_ref[0:1, :], mod_ref[1:2, :], mod_ref[2:3, :]

    if temporal:
        length = length_ref[0]
        key = lax.broadcasted_iota(jnp.int32, (T, T), 0)
        query = lax.broadcasted_iota(jnp.int32, (T, T), 1)
        live = ((key & 15) == (query & 15)) & (key < length * 16)
        mask[...] = jnp.where(live, 1.0, 0.0)

    def norm_rows(i, _):
        at = pl.ds(pl.multiple_of(i * 128, 128), 128)
        x = tokens_ref[at, :].astype(jnp.float32)
        center = x - jnp.mean(x, axis=-1, keepdims=True)
        spread = jnp.mean(center * center, axis=-1, keepdims=True)
        h = center * lax.rsqrt(spread + EPSILON) * (1.0 + stretch) + offset
        hidden[:, at] = h.T.astype(jnp.bfloat16)
        return 0

    lax.fori_loop(0, T // 128, norm_rows, 0)

    group = 8

    def project(i, _):
        rows = weights_ref[pl.ds(i * group, group)].reshape(group * ROWS, D)
        out = jnp.dot(rows, hidden[...], preferred_element_type=jnp.float32)
        for j in range(group // 2):
            low = out[2 * j * ROWS : 2 * j * ROWS + QKV_ROWS]
            high = out[(2 * j + 1) * ROWS : (2 * j + 1) * ROWS + QKV_ROWS]
            both = jnp.concatenate([low, high], axis=0)
            for m in range(3):
                qkv[i * (3 * group // 2) + 3 * j + m] = both[m * HD : (m + 1) * HD].astype(jnp.bfloat16)
        for j in range(group):
            wo[pl.ds(pl.multiple_of((i * group + j) * 48, 16), 48), :] = weights_ref[i * group + j, 96:144, :]
        return 0

    lax.fori_loop(0, SHARDS // group, project, 0)

    def head_norm(values, column):
        values = values.astype(jnp.float32)
        square = jnp.mean(values * values, axis=0, keepdims=True)
        normed = values * lax.rsqrt(square + EPSILON) * gain_ref[:, column : column + 1]
        if temporal:
            swapped = jnp.concatenate([normed[HD // 2 :], normed[: HD // 2]], axis=0)
            normed = normed * cos_ref[...] + swapped * sin_ref[...]
        return normed

    def head(h, _):
        q = head_norm(qkv[h], 0).astype(jnp.bfloat16)
        k = head_norm(qkv[HEADS + h], 1).T.astype(jnp.bfloat16)
        v = qkv[2 * HEADS + h]
        scores = jnp.dot(k, q, preferred_element_type=jnp.float32)
        exponent = jnp.exp2(scores * SCALE)
        if temporal:
            exponent = exponent * mask[...]
        total = jnp.sum(exponent, axis=0, keepdims=True)
        weights = (exponent * (1.0 / total)).astype(jnp.bfloat16)
        result = jnp.dot(v, weights, preferred_element_type=jnp.float32)
        attended[pl.ds(pl.multiple_of(h * HD, 8), HD), :] = result
        return 0

    lax.fori_loop(0, HEADS, head, 0)
    attended_bf[...] = attended[...].astype(jnp.bfloat16)

    def output(i, _):
        rows = wo[pl.ds(pl.multiple_of(i * 384, 16), 384), :]
        out = jnp.dot(rows, attended_bf[...], preferred_element_type=jnp.float32)
        for j in range(4):
            both = jnp.concatenate([out[96 * j + 12 : 96 * j + 48], out[96 * j + 60 : 96 * j + 96]], axis=0)
            update[pl.ds(pl.multiple_of((i * 4 + j) * 72, 8), 72), :] = both
        return 0

    lax.fori_loop(0, 4, output, 0)

    def finish(i, _):
        at = pl.ds(pl.multiple_of(i * 128, 128), 128)
        value = tokens_ref[at, :].astype(jnp.float32) + gating * update[:, at].T
        if temporal:
            frame = (i * 128 + lax.broadcasted_iota(jnp.int32, (128, 1), 0)) // 16
            value = value * jnp.where(frame < length, 1.0, 0.0)
        out_ref[at, :] = value.astype(jnp.bfloat16)
        return 0

    lax.fori_loop(0, T // 128, finish, 0)


def block(tokens, weights, mod, gain, length=None, tables=()):
    temporal = length is not None
    vmem = pl.BlockSpec(memory_space=pltpu.VMEM)
    operands = [tokens, weights, mod, gain.T, *tables]
    specs = [vmem] * len(operands)
    scratch = [
        pltpu.VMEM((D, T), jnp.bfloat16),
        pltpu.VMEM((3 * HEADS, HD, T), jnp.bfloat16),
        pltpu.VMEM((D, T), jnp.float32),
        pltpu.VMEM((D, T), jnp.bfloat16),
        pltpu.VMEM((SHARDS * 48, D), jnp.bfloat16),
        pltpu.VMEM((D, T), jnp.float32),
    ]
    if temporal:
        operands = [length.reshape(1), *operands]
        specs = [pl.BlockSpec(memory_space=pltpu.SMEM), *specs]
        scratch.append(pltpu.VMEM((T, T), jnp.float32))
    return pl.pallas_call(
        functools.partial(block_kernel, temporal),
        out_shape=jax.ShapeDtypeStruct((T, D), jnp.bfloat16),
        in_specs=specs,
        out_specs=vmem,
        scratch_shapes=scratch,
        compiler_params=pltpu.CompilerParams(vmem_limit_bytes=56 * 1024 * 1024),
        cost_estimate=pl.CostEstimate(flops=9 * 10**9, bytes_accessed=13 * 10**6, transcendentals=4 * 10**6),
    )(*operands)


def rotary_tables():
    frames = jnp.arange(T, dtype=jnp.float32) // 16.0
    frequency = jnp.power(10000.0, -2.0 * jnp.arange(HD // 2, dtype=jnp.float32) / HD)
    angles = frequency[:, None] * frames[None, :]
    cosine, sine = jnp.cos(angles), jnp.sin(angles)
    return jnp.concatenate([cosine, cosine], 0), jnp.concatenate([-sine, sine], 0)


def gather_rows(project, output):
    rows = jnp.concatenate([project.T, output.T], axis=0)
    return lax.all_gather(rows, "seq", axis=0, tiled=False)


def on_device(
    latents,
    sampler_order,
    frame_counts,
    modulation,
    spatial_project,
    spatial_output,
    spatial_gain,
    temporal_project,
    temporal_output,
    temporal_gain,
):
    clip_id = sampler_order[lax.axis_index("group")]
    length = frame_counts[clip_id]
    mod = lax.dynamic_index_in_dim(modulation, clip_id, 0, keepdims=False)
    outgoing = jnp.take(latents, sampler_order, axis=0)
    arrived = lax.all_to_all(outgoing, "group", split_axis=0, concat_axis=2, tiled=True)
    tokens = arrived.reshape(T, D)
    spatial_weights = gather_rows(spatial_project, spatial_output)
    temporal_weights = gather_rows(temporal_project, temporal_output)
    mixture = block(tokens, spatial_weights, mod[0:3], spatial_gain)
    by_position = lax.all_to_all(
        mixture.reshape(SHARDS, T // SHARDS, D), "seq", split_axis=0, concat_axis=0, tiled=True
    )
    finished = block(
        by_position.reshape(T, D), temporal_weights, mod[3:6], temporal_gain, length, rotary_tables()
    )
    returned = lax.all_to_all(
        finished.reshape(SHARDS, T // SHARDS, D), "seq", split_axis=0, concat_axis=0, tiled=True
    )
    return returned.reshape(1, 1, T, D)


def solution(mesh):
    in_specs = (
        P(None, "seq", "group", None),
        P(),
        P(),
        P(),
        P(None, "seq"),
        P(None, "seq"),
        P(),
        P(None, "seq"),
        P(None, "seq"),
        P(),
    )
    out_specs = P("group", "seq", None, None)
    return jax.shard_map(
        on_device, mesh=mesh, in_specs=in_specs, out_specs=out_specs, check_vma=False
    )
```

```python
import functools
import math

import jax
import jax.numpy as jnp
from jax import lax
from jax.experimental import pallas as pl
from jax.experimental.pallas import tpu as pltpu
from jax.sharding import PartitionSpec as P

HEADS = 16
HD = 72
D = 1152
T = 512
SHARDS = 32
QKV_ROWS = 108
OUT_ROWS = 36
ROWS = QKV_ROWS + OUT_ROWS
HALF = 64
EPSILON = 1e-06
SCALE = math.log2(math.e) / math.sqrt(HD)


def block_kernel(temporal, *refs):
    if temporal:
        (length_ref, tokens_ref, weights_ref, mod_ref, gain_ref, cos_ref, sin_ref,
         out_ref, hidden, qkv, attended, attended_bf, wo, update, mask) = refs
    else:
        (tokens_ref, weights_ref, mod_ref, gain_ref,
         out_ref, hidden, qkv, attended, attended_bf, wo, update) = refs

    offset, stretch, gating = mod_ref[0:1, :], mod_ref[1:2, :], mod_ref[2:3, :]

    if temporal:
        length = length_ref[0]
        key = lax.broadcasted_iota(jnp.int32, (T, T), 0)
        query = lax.broadcasted_iota(jnp.int32, (T, T), 1)
        live = ((key & 15) == (query & 15)) & (key < length * 16)
        mask[...] = jnp.where(live, 1.0, 0.0)

    def norm_rows(i, _):
        at = pl.ds(pl.multiple_of(i * 128, 128), 128)
        x = tokens_ref[at, :].astype(jnp.float32)
        center = x - jnp.mean(x, axis=-1, keepdims=True)
        spread = jnp.mean(center * center, axis=-1, keepdims=True)
        h = center * lax.rsqrt(spread + EPSILON) * (1.0 + stretch) + offset
        hidden[:, at] = h.T.astype(jnp.bfloat16)
        return 0

    lax.fori_loop(0, T // 128, norm_rows, 0)

    group = 8

    def project(i, _):
        rows = weights_ref[pl.ds(i * group, group)].reshape(group * ROWS, D)
        out = jnp.dot(rows, hidden[...], preferred_element_type=jnp.float32)
        for j in range(group // 2):
            low = out[2 * j * ROWS : 2 * j * ROWS + QKV_ROWS]
            high = out[(2 * j + 1) * ROWS : (2 * j + 1) * ROWS + QKV_ROWS]
            both = jnp.concatenate([low, high], axis=0)
            for m in range(3):
                qkv[i * (3 * group // 2) + 3 * j + m] = both[m * HD : (m + 1) * HD].astype(jnp.bfloat16)
        for j in range(group):
            wo[pl.ds(pl.multiple_of((i * group + j) * 48, 16), 48), :] = weights_ref[i * group + j, 96:144, :]
        return 0

    lax.fori_loop(0, SHARDS // group, project, 0)

    def head_norm(values, column):
        values = values.astype(jnp.float32)
        square = jnp.mean(values * values, axis=0, keepdims=True)
        normed = values * lax.rsqrt(square + EPSILON) * gain_ref[:, column : column + 1]
        if temporal:
            swapped = jnp.concatenate([normed[HD // 2 :], normed[: HD // 2]], axis=0)
            normed = normed * cos_ref[...] + swapped * sin_ref[...]
        return normed

    def head(h, _):
        q = head_norm(qkv[h], 0).astype(jnp.bfloat16)
        k = head_norm(qkv[HEADS + h], 1).T.astype(jnp.bfloat16)
        v = qkv[2 * HEADS + h]
        scores = jnp.dot(k, q, preferred_element_type=jnp.float32)
        exponent = jnp.exp2(scores * SCALE)
        if temporal:
            exponent = exponent * mask[...]
        total = jnp.sum(exponent, axis=0, keepdims=True)
        weights = (exponent * (1.0 / total)).astype(jnp.bfloat16)
        result = jnp.dot(v, weights, preferred_element_type=jnp.float32)
        attended[pl.ds(pl.multiple_of(h * HD, 8), HD), :] = result
        return 0

    lax.fori_loop(0, HEADS, head, 0)
    attended_bf[...] = attended[...].astype(jnp.bfloat16)

    def output(i, _):
        rows = wo[pl.ds(pl.multiple_of(i * 384, 16), 384), :]
        out = jnp.dot(rows, attended_bf[...], preferred_element_type=jnp.float32)
        for j in range(4):
            both = jnp.concatenate([out[96 * j + 12 : 96 * j + 48], out[96 * j + 60 : 96 * j + 96]], axis=0)
            update[pl.ds(pl.multiple_of((i * 4 + j) * 72, 8), 72), :] = both
        return 0

    lax.fori_loop(0, 4, output, 0)

    def finish(i, _):
        at = pl.ds(pl.multiple_of(i * 128, 128), 128)
        value = tokens_ref[at, :].astype(jnp.float32) + gating * update[:, at].T
        if temporal:
            frame = (i * 128 + lax.broadcasted_iota(jnp.int32, (128, 1), 0)) // 16
            value = value * jnp.where(frame < length, 1.0, 0.0)
        out_ref[at, :] = value.astype(jnp.bfloat16)
        return 0

    lax.fori_loop(0, T // 128, finish, 0)


def block(tokens, weights, mod, gain, length=None, tables=()):
    temporal = length is not None
    vmem = pl.BlockSpec(memory_space=pltpu.VMEM)
    operands = [tokens, weights, mod, gain.T, *tables]
    specs = [vmem] * len(operands)
    scratch = [
        pltpu.VMEM((D, T), jnp.bfloat16),
        pltpu.VMEM((3 * HEADS, HD, T), jnp.bfloat16),
        pltpu.VMEM((D, T), jnp.float32),
        pltpu.VMEM((D, T), jnp.bfloat16),
        pltpu.VMEM((SHARDS * 48, D), jnp.bfloat16),
        pltpu.VMEM((D, T), jnp.float32),
    ]
    if temporal:
        operands = [length.reshape(1), *operands]
        specs = [pl.BlockSpec(memory_space=pltpu.SMEM), *specs]
        scratch.append(pltpu.VMEM((T, T), jnp.float32))
    return pl.pallas_call(
        functools.partial(block_kernel, temporal),
        out_shape=jax.ShapeDtypeStruct((T, D), jnp.bfloat16),
        in_specs=specs,
        out_specs=vmem,
        scratch_shapes=scratch,
        compiler_params=pltpu.CompilerParams(vmem_limit_bytes=56 * 1024 * 1024),
        cost_estimate=pl.CostEstimate(flops=9 * 10**9, bytes_accessed=13 * 10**6, transcendentals=4 * 10**6),
    )(*operands)


def rotary_tables():
    frames = jnp.arange(T, dtype=jnp.float32) // 16.0
    frequency = jnp.power(10000.0, -2.0 * jnp.arange(HD // 2, dtype=jnp.float32) / HD)
    angles = frequency[:, None] * frames[None, :]
    cosine, sine = jnp.cos(angles), jnp.sin(angles)
    return jnp.concatenate([cosine, cosine], 0), jnp.concatenate([-sine, sine], 0)


def gather_kernel(shard_ref, gathered_ref, own_sem, send_sem, recv_sem):
    me = lax.axis_index("seq")
    core = lax.rem(me, 2)
    x, y = me // 8, lax.rem(me // 2, 4)
    first, second = jnp.where(core == 0, x, y), jnp.where(core == 0, y, x)
    first_stride, second_stride = jnp.where(core == 0, 8, 2), jnp.where(core == 0, 2, 8)

    def at(da, db):
        return (
            lax.rem(first + da, 4) * first_stride + lax.rem(second + db, 4) * second_stride + core
        )

    sibling = me + 1 - 2 * core
    a_next, a_back, b_next, b_back = at(1, 0), at(3, 0), at(0, 1), at(0, 3)
    barrier = pltpu.get_barrier_semaphore()
    for other in (sibling, a_next, a_back, b_next, b_back):
        pl.semaphore_signal(
            barrier, inc=1, device_id={"seq": other}, device_id_type=pl.DeviceIdType.MESH
        )
    pl.semaphore_wait(barrier, 5)

    started = []
    low, high = pl.ds(0, HALF), pl.ds(HALF, ROWS - HALF)
    whole = pl.ds(0, ROWS)

    def copy(kind, slot, rows, target, source=None):
        return pltpu.make_async_remote_copy(
            src_ref=gathered_ref.at[slot, rows] if source is None else source,
            dst_ref=gathered_ref.at[slot, rows],
            send_sem=send_sem.at[kind],
            recv_sem=recv_sem.at[kind],
            device_id={"seq": target},
            device_id_type=pl.DeviceIdType.MESH,
        )

    def send(kind, slot, rows, target, source=None):
        made = copy(kind, slot, rows, target, source)
        made.start()
        started.append(made)

    def arrived(kind, slot, rows):
        copy(kind, slot, rows, sibling).wait_recv()

    def along_second(da, source=None):
        send(4 + 4 * da, at(da, 0), whole, b_next, source)
        send(5 + 4 * da, at(da, 0), whole, b_back, source)
        send(20 + 4 * da, at(da, 0), whole, sibling, source)

    def near(da):
        arrived(4 + 4 * da, at(da, 3), whole)
        send(6 + 4 * da, at(da, 3), low, b_next)
        send(20 + 4 * da + 3, at(da, 3), whole, sibling)
        arrived(5 + 4 * da, at(da, 1), whole)
        send(7 + 4 * da, at(da, 1), high, b_back)
        send(20 + 4 * da + 1, at(da, 1), whole, sibling)

    def far(da):
        arrived(6 + 4 * da, at(da, 2), low)
        arrived(7 + 4 * da, at(da, 2), high)
        send(20 + 4 * da + 2, at(da, 2), whole, sibling)

    send(0, me, whole, a_next, shard_ref)
    send(1, me, whole, a_back, shard_ref)
    along_second(0, shard_ref)
    own = pltpu.make_async_copy(shard_ref, gathered_ref.at[me], own_sem)
    own.start()
    arrived(0, at(3, 0), whole)
    send(2, at(3, 0), low, a_next)
    along_second(3)
    arrived(1, at(1, 0), whole)
    send(3, at(1, 0), high, a_back)
    along_second(1)
    near(0)
    arrived(2, at(2, 0), low)
    arrived(3, at(2, 0), high)
    along_second(2)
    near(3)
    near(1)
    far(0)
    near(2)
    far(3)
    far(1)
    far(2)
    for da in range(4):
        for db in range(4):
            mine = (
                lax.rem(second + da, 4) * second_stride
                + lax.rem(first + db, 4) * first_stride
                + 1
                - core
            )
            arrived(20 + 4 * da + db, mine, whole)
    for made in started:
        made.wait_send()
    own.wait()


def gather_fast(rows):
    anywhere = pl.BlockSpec(memory_space=pl.ANY)
    return pl.pallas_call(
        gather_kernel,
        out_shape=jax.ShapeDtypeStruct((SHARDS, ROWS, D), jnp.bfloat16),
        in_specs=[anywhere],
        out_specs=anywhere,
        scratch_shapes=[
            pltpu.SemaphoreType.DMA,
            pltpu.SemaphoreType.DMA((36,)),
            pltpu.SemaphoreType.DMA((36,)),
        ],
        compiler_params=pltpu.CompilerParams(collective_id=0, has_side_effects=True),
        cost_estimate=pl.CostEstimate(flops=0, bytes_accessed=60 * 10**6, transcendentals=0),
    )(rows)


def shard_rows(project, output):
    return jnp.concatenate([project.T, output.T], axis=0)


def on_device(
    latents,
    sampler_order,
    frame_counts,
    modulation,
    spatial_project,
    spatial_output,
    spatial_gain,
    temporal_project,
    temporal_output,
    temporal_gain,
):
    clip_id = sampler_order[lax.axis_index("group")]
    length = frame_counts[clip_id]
    mod = lax.dynamic_index_in_dim(modulation, clip_id, 0, keepdims=False)
    outgoing = jnp.take(latents, sampler_order, axis=0)
    arrived = lax.all_to_all(outgoing, "group", split_axis=0, concat_axis=2, tiled=True)
    tokens = arrived.reshape(T, D)
    spatial_weights = gather_fast(shard_rows(spatial_project, spatial_output))
    temporal_weights = lax.all_gather(
        shard_rows(temporal_project, temporal_output), "seq", axis=0, tiled=False
    )
    mixture = block(tokens, spatial_weights, mod[0:3], spatial_gain)
    by_position = lax.all_to_all(
        mixture.reshape(SHARDS, T // SHARDS, D), "seq", split_axis=0, concat_axis=0, tiled=True
    )
    finished = block(
        by_position.reshape(T, D), temporal_weights, mod[3:6], temporal_gain, length, rotary_tables()
    )
    returned = lax.all_to_all(
        finished.reshape(SHARDS, T // SHARDS, D), "seq", split_axis=0, concat_axis=0, tiled=True
    )
    return returned.reshape(1, 1, T, D)


def solution(mesh):
    in_specs = (
        P(None, "seq", "group", None),
        P(),
        P(),
        P(),
        P(None, "seq"),
        P(None, "seq"),
        P(),
        P(None, "seq"),
        P(None, "seq"),
        P(),
    )
    out_specs = P("group", "seq", None, None)
    return jax.shard_map(
        on_device, mesh=mesh, in_specs=in_specs, out_specs=out_specs, check_vma=False
    )
```

```python
import functools
import math

import jax
import jax.numpy as jnp
from jax import lax
from jax.experimental import pallas as pl
from jax.experimental.pallas import tpu as pltpu
from jax.sharding import PartitionSpec as P

HEADS = 16
HD = 72
D = 1152
T = 512
SHARDS = 32
QKV_ROWS = 108
OUT_ROWS = 36
ROWS = QKV_ROWS + OUT_ROWS
HALF = 64
EPSILON = 1e-06
SCALE = math.log2(math.e) / math.sqrt(HD)


def block_kernel(temporal, *refs):
    if temporal:
        (length_ref, tokens_ref, held_ref, mod_ref, gain_ref, cos_ref, sin_ref,
         out_ref, weights_ref, load_sem,
         hidden, qkv, attended, attended_bf, wo, update, mask) = refs
        pump = iter(())
    else:
        (tokens_ref, held_ref, mod_ref, gain_ref, shard_ref,
         out_ref, gathered_ref, weights_ref, load_sem,
         hidden, qkv, attended, attended_bf, wo, update, own_sem, send_sem, recv_sem) = refs

    group = 8
    loads = []
    for i in range(SHARDS // group):
        part = pl.ds(i * group, group)
        loads.append(
            pltpu.make_async_copy(held_ref.at[part], weights_ref.at[part], load_sem.at[i])
        )
        loads[-1].start()

    if not temporal:
        greet(seq_neighbours())
        pump = gather_steps(shard_ref, gathered_ref, own_sem, send_sem, recv_sem)
        next(pump)

    def advance(count):
        for _ in range(count):
            next(pump, None)

    offset, stretch, gating = mod_ref[0:1, :], mod_ref[1:2, :], mod_ref[2:3, :]

    if temporal:
        length = length_ref[0]
        key = lax.broadcasted_iota(jnp.int32, (T, T), 0)
        query = lax.broadcasted_iota(jnp.int32, (T, T), 1)
        live = ((key & 15) == (query & 15)) & (key < length * 16)
        mask[...] = jnp.where(live, 1.0, 0.0)

    def norm_rows(i, _):
        at = pl.ds(pl.multiple_of(i * 128, 128), 128)
        x = tokens_ref[at, :].astype(jnp.float32)
        center = x - jnp.mean(x, axis=-1, keepdims=True)
        spread = jnp.mean(center * center, axis=-1, keepdims=True)
        h = center * lax.rsqrt(spread + EPSILON) * (1.0 + stretch) + offset
        hidden[:, at] = h.T.astype(jnp.bfloat16)
        return 0

    lax.fori_loop(0, T // 128, norm_rows, 0)

    def project(i, _):
        rows = weights_ref[pl.ds(i * group, group)].reshape(group * ROWS, D)
        out = jnp.dot(rows, hidden[...], preferred_element_type=jnp.float32)
        for j in range(group // 2):
            low = out[2 * j * ROWS : 2 * j * ROWS + QKV_ROWS]
            high = out[(2 * j + 1) * ROWS : (2 * j + 1) * ROWS + QKV_ROWS]
            both = jnp.concatenate([low, high], axis=0)
            for m in range(3):
                qkv[i * (3 * group // 2) + 3 * j + m] = both[m * HD : (m + 1) * HD].astype(jnp.bfloat16)
        for j in range(group):
            wo[pl.ds((i * group + j) * 48, 48), :] = weights_ref[i * group + j, 96:144, :]
        return 0

    for i in range(SHARDS // group):
        loads[i].wait()
        project(i, 0)
        advance(2)

    def head_norm(values, column):
        values = values.astype(jnp.float32)
        square = jnp.mean(values * values, axis=0, keepdims=True)
        normed = values * lax.rsqrt(square + EPSILON) * gain_ref[:, column : column + 1]
        if temporal:
            swapped = jnp.concatenate([normed[HD // 2 :], normed[: HD // 2]], axis=0)
            normed = normed * cos_ref[...] + swapped * sin_ref[...]
        return normed

    def head(h, _):
        q = head_norm(qkv[h], 0).astype(jnp.bfloat16)
        k = head_norm(qkv[HEADS + h], 1).T.astype(jnp.bfloat16)
        v = qkv[2 * HEADS + h]
        scores = jnp.dot(k, q, preferred_element_type=jnp.float32)
        exponent = jnp.exp2(scores * SCALE)
        if temporal:
            exponent = exponent * mask[...]
        total = jnp.sum(exponent, axis=0, keepdims=True)
        weights = (exponent * (1.0 / total)).astype(jnp.bfloat16)
        result = jnp.dot(v, weights, preferred_element_type=jnp.float32)
        attended[pl.ds(pl.multiple_of(h * HD, 8), HD), :] = result
        return 0

    if temporal:
        lax.fori_loop(0, HEADS, head, 0, unroll=4)
    else:
        for i in range(4):
            lax.fori_loop(4 * i, 4 * i + 4, head, 0, unroll=2)
            advance(2)
    attended_bf[...] = attended[...].astype(jnp.bfloat16)

    def output(i, _):
        rows = wo[pl.ds(i * 384, 384), :]
        out = jnp.dot(rows, attended_bf[...], preferred_element_type=jnp.float32)
        for j in range(4):
            both = jnp.concatenate([out[96 * j + 12 : 96 * j + 48], out[96 * j + 60 : 96 * j + 96]], axis=0)
            update[pl.ds((i * 4 + j) * 72, 72), :] = both
        return 0

    for i in range(4):
        output(i, 0)
        advance(1)

    def finish(i, _):
        at = pl.ds(pl.multiple_of(i * 128, 128), 128)
        value = tokens_ref[at, :].astype(jnp.float32) + gating * update[:, at].T
        if temporal:
            frame = (i * 128 + lax.broadcasted_iota(jnp.int32, (128, 1), 0)) // 16
            value = value * jnp.where(frame < length, 1.0, 0.0)
        out_ref[at, :] = value.astype(jnp.bfloat16)
        return 0

    lax.fori_loop(0, T // 128, finish, 0)
    for _ in pump:
        pass


GATHER_SCRATCH = [
    pltpu.SemaphoreType.DMA,
    pltpu.SemaphoreType.DMA((36,)),
    pltpu.SemaphoreType.DMA((36,)),
]


def block(tokens, weights, mod, gain, length=None, tables=(), shard=None):
    temporal = length is not None
    vmem = pl.BlockSpec(memory_space=pltpu.VMEM)
    anywhere = pl.BlockSpec(memory_space=pl.ANY)
    operands = [tokens, weights, mod, gain.T]
    specs = [vmem, anywhere, vmem, vmem]
    out_shape = jax.ShapeDtypeStruct((T, D), jnp.bfloat16)
    out_specs = vmem
    params = dict(vmem_limit_bytes=56 * 1024 * 1024)
    scratch = [
        pltpu.VMEM((SHARDS, ROWS, D), jnp.bfloat16),
        pltpu.SemaphoreType.DMA((4,)),
        pltpu.VMEM((D, T), jnp.bfloat16),
        pltpu.VMEM((3 * HEADS, HD, T), jnp.bfloat16),
        pltpu.VMEM((D, T), jnp.float32),
        pltpu.VMEM((D, T), jnp.bfloat16),
        pltpu.VMEM((SHARDS * 48, D), jnp.bfloat16),
        pltpu.VMEM((D, T), jnp.float32),
    ]
    if temporal:
        operands = [length.reshape(1), *operands, *tables]
        specs = [pl.BlockSpec(memory_space=pltpu.SMEM), *specs, vmem, vmem]
        scratch.append(pltpu.VMEM((T, T), jnp.float32))
    else:
        operands.append(shard)
        specs.append(anywhere)
        out_shape = (out_shape, jax.ShapeDtypeStruct((SHARDS, ROWS, D), jnp.bfloat16))
        out_specs = (out_specs, anywhere)
        scratch += GATHER_SCRATCH
        params.update(collective_id=1, has_side_effects=True)
    return pl.pallas_call(
        functools.partial(block_kernel, temporal),
        out_shape=out_shape,
        in_specs=specs,
        out_specs=out_specs,
        scratch_shapes=scratch,
        compiler_params=pltpu.CompilerParams(**params),
        cost_estimate=pl.CostEstimate(flops=9 * 10**9, bytes_accessed=13 * 10**6, transcendentals=4 * 10**6),
    )(*operands)


def rotary_tables():
    frames = jnp.arange(T, dtype=jnp.float32) // 16.0
    frequency = jnp.power(10000.0, -2.0 * jnp.arange(HD // 2, dtype=jnp.float32) / HD)
    angles = frequency[:, None] * frames[None, :]
    cosine, sine = jnp.cos(angles), jnp.sin(angles)
    return jnp.concatenate([cosine, cosine], 0), jnp.concatenate([-sine, sine], 0)


MESH = pl.DeviceIdType.MESH


def seq_place():
    me = lax.axis_index("seq")
    core = lax.rem(me, 2)
    x, y = me // 8, lax.rem(me // 2, 4)
    first, second = jnp.where(core == 0, x, y), jnp.where(core == 0, y, x)
    first_stride, second_stride = jnp.where(core == 0, 8, 2), jnp.where(core == 0, 2, 8)
    return me, core, first, second, first_stride, second_stride


def seq_neighbours():
    me, core, first, second, first_stride, second_stride = seq_place()

    def at(da, db):
        return (
            lax.rem(first + da, 4) * first_stride + lax.rem(second + db, 4) * second_stride + core
        )

    return [{"seq": i} for i in (me + 1 - 2 * core, at(1, 0), at(3, 0), at(0, 1), at(0, 3))]


def greet(others):
    barrier = pltpu.get_barrier_semaphore()
    for other in others:
        pl.semaphore_signal(barrier, inc=1, device_id=other, device_id_type=MESH)
    pl.semaphore_wait(barrier, len(others))


def gather_steps(shard_ref, gathered_ref, own_sem, send_sem, recv_sem):
    me, core, first, second, first_stride, second_stride = seq_place()

    def at(da, db):
        return (
            lax.rem(first + da, 4) * first_stride + lax.rem(second + db, 4) * second_stride + core
        )

    sibling = me + 1 - 2 * core
    a_next, a_back, b_next, b_back = at(1, 0), at(3, 0), at(0, 1), at(0, 3)
    started = []
    low, high = pl.ds(0, HALF), pl.ds(HALF, ROWS - HALF)
    whole = pl.ds(0, ROWS)

    def copy(kind, slot, rows, target, source=None):
        return pltpu.make_async_remote_copy(
            src_ref=gathered_ref.at[slot, rows] if source is None else source,
            dst_ref=gathered_ref.at[slot, rows],
            send_sem=send_sem.at[kind],
            recv_sem=recv_sem.at[kind],
            device_id={"seq": target},
            device_id_type=MESH,
        )

    def send(kind, slot, rows, target, source=None):
        made = copy(kind, slot, rows, target, source)
        made.start()
        started.append(made)

    def arrived(kind, slot, rows):
        copy(kind, slot, rows, sibling).wait_recv()

    def along_second(da, source=None):
        send(4 + 4 * da, at(da, 0), whole, b_next, source)
        send(5 + 4 * da, at(da, 0), whole, b_back, source)
        send(20 + 4 * da, at(da, 0), whole, sibling, source)

    def near(da):
        arrived(4 + 4 * da, at(da, 3), whole)
        send(6 + 4 * da, at(da, 3), low, b_next)
        send(20 + 4 * da + 3, at(da, 3), whole, sibling)
        yield
        arrived(5 + 4 * da, at(da, 1), whole)
        send(7 + 4 * da, at(da, 1), high, b_back)
        send(20 + 4 * da + 1, at(da, 1), whole, sibling)
        yield

    def far(da):
        arrived(6 + 4 * da, at(da, 2), low)
        arrived(7 + 4 * da, at(da, 2), high)
        send(20 + 4 * da + 2, at(da, 2), whole, sibling)
        yield

    send(0, me, whole, a_next, shard_ref)
    send(1, me, whole, a_back, shard_ref)
    along_second(0, shard_ref)
    own = pltpu.make_async_copy(shard_ref, gathered_ref.at[me], own_sem)
    own.start()
    yield
    arrived(0, at(3, 0), whole)
    send(2, at(3, 0), low, a_next)
    along_second(3)
    yield
    arrived(1, at(1, 0), whole)
    send(3, at(1, 0), high, a_back)
    along_second(1)
    yield
    yield from near(0)
    arrived(2, at(2, 0), low)
    arrived(3, at(2, 0), high)
    along_second(2)
    yield
    yield from near(3)
    yield from near(1)
    yield from far(0)
    yield from near(2)
    yield from far(3)
    yield from far(1)
    yield from far(2)
    for da in range(4):
        for db in range(4):
            mine = (
                lax.rem(second + da, 4) * second_stride
                + lax.rem(first + db, 4) * first_stride
                + 1
                - core
            )
            arrived(20 + 4 * da + db, mine, whole)
    for made in started:
        made.wait_send()
    own.wait()


def first_kernel(shard_ref, outgoing_ref, gathered_ref, tokens_ref,
                 own_sem, send_sem, recv_sem, keep_sem, out_sem, in_sem):
    here = lax.axis_index("group")
    clips = outgoing_ref.shape[0]
    peers = [lax.rem(here + d, clips) for d in range(1, clips)]
    greet(seq_neighbours() + [{"group": peer} for peer in peers])
    keep = pltpu.make_async_copy(outgoing_ref.at[here], tokens_ref.at[here], keep_sem)
    keep.start()
    sent = []
    for d in range(1, clips):
        sent.append(
            pltpu.make_async_remote_copy(
                src_ref=outgoing_ref.at[peers[d - 1]],
                dst_ref=tokens_ref.at[here],
                send_sem=out_sem.at[d - 1],
                recv_sem=in_sem.at[d - 1],
                device_id={"group": peers[d - 1]},
                device_id_type=MESH,
            )
        )
        sent[-1].start()
    for _ in gather_steps(shard_ref, gathered_ref, own_sem, send_sem, recv_sem):
        pass
    for made in sent:
        made.wait()
    keep.wait()


def first_exchange(rows, outgoing):
    anywhere = pl.BlockSpec(memory_space=pl.ANY)
    clips = outgoing.shape[0]
    return pl.pallas_call(
        first_kernel,
        out_shape=(
            jax.ShapeDtypeStruct((SHARDS, ROWS, D), jnp.bfloat16),
            jax.ShapeDtypeStruct(outgoing.shape, outgoing.dtype),
        ),
        in_specs=[anywhere] * 2,
        out_specs=(anywhere, anywhere),
        scratch_shapes=GATHER_SCRATCH
        + [
            pltpu.SemaphoreType.DMA,
            pltpu.SemaphoreType.DMA((clips - 1,)),
            pltpu.SemaphoreType.DMA((clips - 1,)),
        ],
        compiler_params=pltpu.CompilerParams(collective_id=0, has_side_effects=True),
        cost_estimate=pl.CostEstimate(flops=0, bytes_accessed=60 * 10**6, transcendentals=0),
    )(rows, outgoing)


def shard_rows(project, output):
    return jnp.concatenate([project.T, output.T], axis=0)


def on_device(
    latents,
    sampler_order,
    frame_counts,
    modulation,
    spatial_project,
    spatial_output,
    spatial_gain,
    temporal_project,
    temporal_output,
    temporal_gain,
):
    clip_id = sampler_order[lax.axis_index("group")]
    length = frame_counts[clip_id]
    mod = lax.dynamic_index_in_dim(modulation, clip_id, 0, keepdims=False)
    outgoing = jnp.take(latents, sampler_order, axis=0).reshape(-1, latents.shape[2], D)
    spatial_weights, arrived = first_exchange(
        shard_rows(spatial_project, spatial_output), outgoing
    )
    mixture, temporal_weights = block(
        arrived.reshape(T, D),
        spatial_weights,
        mod[0:3],
        spatial_gain,
        shard=shard_rows(temporal_project, temporal_output),
    )
    by_position = lax.all_to_all(
        mixture.reshape(SHARDS, T // SHARDS, D), "seq", split_axis=0, concat_axis=0, tiled=True
    )
    finished = block(
        by_position.reshape(T, D), temporal_weights, mod[3:6], temporal_gain, length, rotary_tables()
    )
    returned = lax.all_to_all(
        finished.reshape(SHARDS, T // SHARDS, D), "seq", split_axis=0, concat_axis=0, tiled=True
    )
    return returned.reshape(1, 1, T, D)


def solution(mesh):
    in_specs = (
        P(None, "seq", "group", None),
        P(),
        P(),
        P(),
        P(None, "seq"),
        P(None, "seq"),
        P(),
        P(None, "seq"),
        P(None, "seq"),
        P(),
    )
    out_specs = P("group", "seq", None, None)
    return jax.shard_map(
        on_device, mesh=mesh, in_specs=in_specs, out_specs=out_specs, check_vma=False
    )
```

```python
import functools
import math

import jax
import jax.numpy as jnp
from jax import lax
from jax.experimental import pallas as pl
from jax.experimental.pallas import tpu as pltpu
from jax.sharding import PartitionSpec as P

HEADS = 16
HD = 72
D = 1152
T = 512
SHARDS = 32
QKV_ROWS = 108
OUT_ROWS = 36
ROWS = QKV_ROWS + OUT_ROWS
MAIN = 112
REST = ROWS - MAIN
EPSILON = 1e-06
SCALE = math.log2(math.e) / math.sqrt(HD)


def block_kernel(temporal, *refs):
    tokens_ref, held_ref, rest_ref, mod_ref, gain_ref, *refs = refs
    if temporal:
        live_ref, cos_ref, sin_ref, out_ref, *refs = refs
    else:
        shard_ref, out_ref, gathered_ref, *refs = refs
    (weights_ref, rests_ref, load_sem, own_sem, send_sem, recv_sem,
     hidden, qkv, attended, attended_bf, wo, update, *refs) = refs

    group = 8
    loads = []
    for i in range(SHARDS // group):
        part = pl.ds(i * group, group)
        loads.append(
            pltpu.make_async_copy(held_ref.at[part], weights_ref.at[part], load_sem.at[i])
        )
        loads[-1].start()

    greet(seq_neighbours())
    pump_rest = gather_steps(rest_ref, rests_ref, own_sem, send_sem, recv_sem)
    next(pump_rest)
    if temporal:
        (mask,) = refs
        pump = iter(())
    else:
        pump = gather_steps(shard_ref, gathered_ref, *refs)
        next(pump)

    def advance(steps, count):
        for _ in range(count):
            next(steps, None)

    base = 3 if temporal else 0
    offset, stretch, gating = (
        mod_ref[base + i : base + i + 1, :] for i in range(3)
    )
    gain = gain_ref[...].T

    if temporal:
        key = lax.broadcasted_iota(jnp.int32, (T, T), 0)
        query = lax.broadcasted_iota(jnp.int32, (T, T), 1)
        mask[...] = jnp.where((key & 15) == (query & 15), live_ref[...], 0.0)

    def norm_rows(i, _):
        at = pl.ds(pl.multiple_of(i * 128, 128), 128)
        x = tokens_ref[at, :].astype(jnp.float32)
        center = x - jnp.mean(x, axis=-1, keepdims=True)
        spread = jnp.mean(center * center, axis=-1, keepdims=True)
        h = center * lax.rsqrt(spread + EPSILON) * (1.0 + stretch) + offset
        hidden[:, at] = h.T.astype(jnp.bfloat16)
        return 0

    lax.fori_loop(0, T // 128, norm_rows, 0)

    def project(i, _):
        rows = weights_ref[pl.ds(i * group, group)].reshape(group * MAIN, D)
        out = jnp.dot(rows, hidden[...], preferred_element_type=jnp.float32)
        for j in range(group // 2):
            low = out[2 * j * MAIN : 2 * j * MAIN + QKV_ROWS]
            high = out[(2 * j + 1) * MAIN : (2 * j + 1) * MAIN + QKV_ROWS]
            both = jnp.concatenate([low, high], axis=0)
            for m in range(3):
                qkv[i * (3 * group // 2) + 3 * j + m] = both[m * HD : (m + 1) * HD].astype(jnp.bfloat16)
        for j in range(group):
            wo[pl.ds((i * group + j) * 48, 16), :] = weights_ref[i * group + j, 96:MAIN, :]
        return 0

    for i in range(SHARDS // group):
        loads[i].wait()
        project(i, 0)
        advance(pump_rest, 2)
        advance(pump, 1)

    def head_norm(values, column):
        values = values.astype(jnp.float32)
        square = jnp.mean(values * values, axis=0, keepdims=True)
        normed = values * lax.rsqrt(square + EPSILON) * gain[:, column : column + 1]
        if temporal:
            swapped = jnp.concatenate([normed[HD // 2 :], normed[: HD // 2]], axis=0)
            normed = normed * cos_ref[...] + swapped * sin_ref[...]
        return normed

    def head(h, _):
        q = head_norm(qkv[h], 0).astype(jnp.bfloat16)
        k = head_norm(qkv[HEADS + h], 1).T.astype(jnp.bfloat16)
        v = qkv[2 * HEADS + h]
        scores = jnp.dot(k, q, preferred_element_type=jnp.float32)
        exponent = jnp.exp2(scores * SCALE)
        if temporal:
            exponent = exponent * mask[...]
        total = jnp.sum(exponent, axis=0, keepdims=True)
        weights = (exponent * (1.0 / total)).astype(jnp.bfloat16)
        result = jnp.dot(v, weights, preferred_element_type=jnp.float32)
        attended[pl.ds(pl.multiple_of(h * HD, 8), HD), :] = result
        return 0

    for i in range(4):
        lax.fori_loop(4 * i, 4 * i + 4, head, 0, unroll=2)
        advance(pump_rest, 3)
        advance(pump, 2)
    for _ in pump_rest:
        pass
    attended_bf[...] = attended[...].astype(jnp.bfloat16)

    def output(i, _):
        for j in range(group):
            wo[pl.ds((i * group + j) * 48 + 16, REST), :] = rests_ref[i * group + j]
        rows = wo[pl.ds(i * 384, 384), :]
        out = jnp.dot(rows, attended_bf[...], preferred_element_type=jnp.float32)
        for j in range(4):
            both = jnp.concatenate([out[96 * j + 12 : 96 * j + 48], out[96 * j + 60 : 96 * j + 96]], axis=0)
            update[pl.ds((i * 4 + j) * 72, 72), :] = both
        return 0

    for i in range(4):
        output(i, 0)
        advance(pump, 1)

    def finish(i, _):
        at = pl.ds(pl.multiple_of(i * 128, 128), 128)
        value = tokens_ref[at, :].astype(jnp.float32) + gating * update[:, at].T
        if temporal:
            value = value * live_ref[at, :]
        out_ref[at, :] = value.astype(jnp.bfloat16)
        return 0

    lax.fori_loop(0, T // 128, finish, 0)
    for _ in pump:
        pass


GATHER_SCRATCH = [
    pltpu.SemaphoreType.DMA,
    pltpu.SemaphoreType.DMA((36,)),
    pltpu.SemaphoreType.DMA((36,)),
]


def block(tokens, weights, rest, mod, gain, shard=None, tables=()):
    temporal = shard is None
    vmem = pl.BlockSpec(memory_space=pltpu.VMEM)
    anywhere = pl.BlockSpec(memory_space=pl.ANY)
    operands = [tokens, weights, rest, mod, gain]
    specs = [vmem, anywhere, anywhere, vmem, vmem]
    out_shape = jax.ShapeDtypeStruct((T, D), jnp.bfloat16)
    out_specs = vmem
    scratch = [
        pltpu.VMEM((SHARDS, MAIN, D), jnp.bfloat16),
        pltpu.VMEM((SHARDS, REST, D), jnp.bfloat16),
        pltpu.SemaphoreType.DMA((4,)),
        *GATHER_SCRATCH,
        pltpu.VMEM((D, T), jnp.bfloat16),
        pltpu.VMEM((3 * HEADS, HD, T), jnp.bfloat16),
        pltpu.VMEM((D, T), jnp.float32),
        pltpu.VMEM((D, T), jnp.bfloat16),
        pltpu.VMEM((SHARDS * 48, D), jnp.bfloat16),
        pltpu.VMEM((D, T), jnp.float32),
    ]
    if temporal:
        operands += tables
        specs += [vmem] * 3
        scratch.append(pltpu.VMEM((T, T), jnp.float32))
    else:
        operands.append(shard)
        specs.append(anywhere)
        out_shape = (out_shape, jax.ShapeDtypeStruct((SHARDS, MAIN, D), jnp.bfloat16))
        out_specs = (out_specs, anywhere)
        scratch += GATHER_SCRATCH
    return pl.pallas_call(
        functools.partial(block_kernel, temporal),
        out_shape=out_shape,
        in_specs=specs,
        out_specs=out_specs,
        scratch_shapes=scratch,
        compiler_params=pltpu.CompilerParams(
            vmem_limit_bytes=56 * 1024 * 1024,
            collective_id=2 if temporal else 1,
            has_side_effects=True,
        ),
        cost_estimate=pl.CostEstimate(flops=9 * 10**9, bytes_accessed=13 * 10**6, transcendentals=4 * 10**6),
    )(*operands)


def rotary_tables():
    frames = jnp.arange(T, dtype=jnp.float32) // 16.0
    frequency = jnp.power(10000.0, -2.0 * jnp.arange(HD // 2, dtype=jnp.float32) / HD)
    angles = frequency[:, None] * frames[None, :]
    cosine, sine = jnp.cos(angles), jnp.sin(angles)
    return jnp.concatenate([cosine, cosine], 0), jnp.concatenate([-sine, sine], 0)


MESH = pl.DeviceIdType.MESH


def seq_place():
    me = lax.axis_index("seq")
    core = lax.rem(me, 2)
    x, y = me // 8, lax.rem(me // 2, 4)
    first, second = jnp.where(core == 0, x, y), jnp.where(core == 0, y, x)
    first_stride, second_stride = jnp.where(core == 0, 8, 2), jnp.where(core == 0, 2, 8)
    return me, core, first, second, first_stride, second_stride


def seq_neighbours():
    me, core, first, second, first_stride, second_stride = seq_place()

    def at(da, db):
        return (
            lax.rem(first + da, 4) * first_stride + lax.rem(second + db, 4) * second_stride + core
        )

    return [{"seq": i} for i in (me + 1 - 2 * core, at(1, 0), at(3, 0), at(0, 1), at(0, 3))]


def greet(others):
    barrier = pltpu.get_barrier_semaphore()
    for other in others:
        pl.semaphore_signal(barrier, inc=1, device_id=other, device_id_type=MESH)
    pl.semaphore_wait(barrier, len(others))


def gather_steps(shard_ref, gathered_ref, own_sem, send_sem, recv_sem):
    me, core, first, second, first_stride, second_stride = seq_place()

    def at(da, db):
        return (
            lax.rem(first + da, 4) * first_stride + lax.rem(second + db, 4) * second_stride + core
        )

    sibling = me + 1 - 2 * core
    a_next, a_back, b_next, b_back = at(1, 0), at(3, 0), at(0, 1), at(0, 3)
    started = []
    count = shard_ref.shape[0]
    half = count // 32 * 16
    low, high, whole = pl.ds(0, half), pl.ds(half, count - half), pl.ds(0, count)

    def copy(kind, slot, rows, target, source=None):
        return pltpu.make_async_remote_copy(
            src_ref=gathered_ref.at[slot, rows] if source is None else source,
            dst_ref=gathered_ref.at[slot, rows],
            send_sem=send_sem.at[kind],
            recv_sem=recv_sem.at[kind],
            device_id={"seq": target},
            device_id_type=MESH,
        )

    def send(kind, slot, rows, target, source=None):
        made = copy(kind, slot, rows, target, source)
        made.start()
        started.append(made)

    def arrived(kind, slot, rows):
        copy(kind, slot, rows, sibling).wait_recv()

    def along_second(da, source=None):
        send(4 + 4 * da, at(da, 0), whole, b_next, source)
        send(5 + 4 * da, at(da, 0), whole, b_back, source)
        send(20 + 4 * da, at(da, 0), whole, sibling, source)

    def near(da):
        arrived(4 + 4 * da, at(da, 3), whole)
        send(6 + 4 * da, at(da, 3), low, b_next)
        send(20 + 4 * da + 3, at(da, 3), whole, sibling)
        yield
        arrived(5 + 4 * da, at(da, 1), whole)
        send(7 + 4 * da, at(da, 1), high, b_back)
        send(20 + 4 * da + 1, at(da, 1), whole, sibling)
        yield

    def far(da):
        arrived(6 + 4 * da, at(da, 2), low)
        arrived(7 + 4 * da, at(da, 2), high)
        send(20 + 4 * da + 2, at(da, 2), whole, sibling)
        yield

    send(0, me, whole, a_next, shard_ref)
    send(1, me, whole, a_back, shard_ref)
    along_second(0, shard_ref)
    own = pltpu.make_async_copy(shard_ref, gathered_ref.at[me], own_sem)
    own.start()
    yield
    arrived(0, at(3, 0), whole)
    send(2, at(3, 0), low, a_next)
    along_second(3)
    yield
    arrived(1, at(1, 0), whole)
    send(3, at(1, 0), high, a_back)
    along_second(1)
    yield
    yield from near(0)
    arrived(2, at(2, 0), low)
    arrived(3, at(2, 0), high)
    along_second(2)
    yield
    yield from near(3)
    yield from near(1)
    yield from far(0)
    yield from near(2)
    yield from far(3)
    yield from far(1)
    yield from far(2)
    for da in range(4):
        for db in range(4):
            mine = (
                lax.rem(second + da, 4) * second_stride
                + lax.rem(first + db, 4) * first_stride
                + 1
                - core
            )
            arrived(20 + 4 * da + db, mine, whole)
    for made in started:
        made.wait_send()
    own.wait()


def first_kernel(shard_ref, outgoing_ref, gathered_ref, tokens_ref,
                 own_sem, send_sem, recv_sem, keep_sem, out_sem, in_sem):
    here = lax.axis_index("group")
    clips = outgoing_ref.shape[0]
    peers = [lax.rem(here + d, clips) for d in range(1, clips)]
    greet(seq_neighbours() + [{"group": peer} for peer in peers])
    keep = pltpu.make_async_copy(outgoing_ref.at[here], tokens_ref.at[here], keep_sem)
    keep.start()
    sent = []
    for d in range(1, clips):
        sent.append(
            pltpu.make_async_remote_copy(
                src_ref=outgoing_ref.at[peers[d - 1]],
                dst_ref=tokens_ref.at[here],
                send_sem=out_sem.at[d - 1],
                recv_sem=in_sem.at[d - 1],
                device_id={"group": peers[d - 1]},
                device_id_type=MESH,
            )
        )
        sent[-1].start()
    for _ in gather_steps(shard_ref, gathered_ref, own_sem, send_sem, recv_sem):
        pass
    for made in sent:
        made.wait()
    keep.wait()


def first_exchange(rows, outgoing):
    anywhere = pl.BlockSpec(memory_space=pl.ANY)
    clips = outgoing.shape[0]
    return pl.pallas_call(
        first_kernel,
        out_shape=(
            jax.ShapeDtypeStruct((SHARDS, MAIN, D), jnp.bfloat16),
            jax.ShapeDtypeStruct(outgoing.shape, outgoing.dtype),
        ),
        in_specs=[anywhere] * 2,
        out_specs=(anywhere, anywhere),
        scratch_shapes=GATHER_SCRATCH
        + [
            pltpu.SemaphoreType.DMA,
            pltpu.SemaphoreType.DMA((clips - 1,)),
            pltpu.SemaphoreType.DMA((clips - 1,)),
        ],
        compiler_params=pltpu.CompilerParams(collective_id=0, has_side_effects=True),
        cost_estimate=pl.CostEstimate(flops=0, bytes_accessed=60 * 10**6, transcendentals=0),
    )(rows, outgoing)


def shard_rows(project, output):
    return jnp.concatenate([project.T, output.T], axis=0)


def on_device(
    latents,
    sampler_order,
    frame_counts,
    modulation,
    spatial_project,
    spatial_output,
    spatial_gain,
    temporal_project,
    temporal_output,
    temporal_gain,
):
    clip_id = sampler_order[lax.axis_index("group")]
    length = frame_counts[clip_id]
    mod = lax.dynamic_index_in_dim(modulation, clip_id, 0, keepdims=False)
    outgoing = latents.at[sampler_order].get(mode="promise_in_bounds")
    spatial_rows = shard_rows(spatial_project, spatial_output)
    temporal_rows = shard_rows(temporal_project, temporal_output)
    spatial_weights, arrived = first_exchange(
        spatial_rows[:MAIN], outgoing.reshape(-1, latents.shape[2], D)
    )
    mixture, temporal_weights = block(
        arrived.reshape(T, D),
        spatial_weights,
        spatial_rows[MAIN:],
        mod,
        spatial_gain,
        shard=temporal_rows[:MAIN],
    )
    by_position = lax.all_to_all(
        mixture.reshape(SHARDS, T // SHARDS, D), "seq", split_axis=0, concat_axis=0, tiled=True
    )
    live = (jnp.arange(T, dtype=jnp.int32)[:, None] // 16 < length).astype(jnp.float32)
    finished = block(
        by_position.reshape(T, D),
        temporal_weights,
        temporal_rows[MAIN:],
        mod,
        temporal_gain,
        tables=(live, *rotary_tables()),
    )
    returned = lax.all_to_all(
        finished.reshape(SHARDS, T // SHARDS, D), "seq", split_axis=0, concat_axis=0, tiled=True
    )
    return returned.reshape(1, 1, T, D)


def solution(mesh):
    in_specs = (
        P(None, "seq", "group", None),
        P(),
        P(),
        P(),
        P(None, "seq"),
        P(None, "seq"),
        P(),
        P(None, "seq"),
        P(None, "seq"),
        P(),
    )
    out_specs = P("group", "seq", None, None)
    return jax.shard_map(
        on_device, mesh=mesh, in_specs=in_specs, out_specs=out_specs, check_vma=False
    )
```

```python
import functools
import math

import jax
import jax.numpy as jnp
from jax import lax
from jax.experimental import pallas as pl
from jax.experimental.pallas import tpu as pltpu
from jax.sharding import PartitionSpec as P

HEADS = 16
HD = 72
D = 1152
T = 512
SHARDS = 32
QKV_ROWS = 108
OUT_ROWS = 36
ROWS = QKV_ROWS + OUT_ROWS
MAIN = 112
REST = ROWS - MAIN
SEGMENTS = 4
PER_SEGMENT = 2
PER_SEGMENT_T = 4
EPSILON = 1e-06
SCALE = math.log2(math.e) / math.sqrt(HD)


def block_kernel(temporal, *refs):
    tokens_ref, held_ref, rest_ref, mod_ref, gain_ref, *refs = refs
    if temporal:
        live_ref, cos_ref, sin_ref, out_ref, *refs = refs
    else:
        shard_ref, out_ref, gathered_ref, *refs = refs
    (weights_ref, rests_ref, load_sem, own_sem, send_sem, recv_sem,
     hidden, qkv, attended, attended_bf, wo, update, *refs) = refs

    group = 8
    loads = []
    for i in range(SHARDS // group):
        part = pl.ds(i * group, group)
        loads.append(
            pltpu.make_async_copy(held_ref.at[part], weights_ref.at[part], load_sem.at[i])
        )
        loads[-1].start()

    greet(seq_neighbours())
    if temporal:
        (mask,) = refs
        pump = gather_steps(rest_ref, rests_ref, own_sem, send_sem, recv_sem)
    else:
        rest_load = pltpu.make_async_copy(rest_ref, rests_ref, load_sem.at[4])
        rest_load.start()
        pump = gather_steps(shard_ref, gathered_ref, own_sem, send_sem, recv_sem)
    next(pump)

    def advance(count):
        for _ in range(count):
            next(pump, None)

    base = 3 if temporal else 0
    offset, stretch, gating = (
        mod_ref[base + i : base + i + 1, :] for i in range(3)
    )
    gain = gain_ref[...].T

    if temporal:
        key = lax.broadcasted_iota(jnp.int32, (T, T), 0)
        query = lax.broadcasted_iota(jnp.int32, (T, T), 1)
        mask[...] = jnp.where((key & 15) == (query & 15), live_ref[...], 0.0)

    def norm_rows(i, _):
        at = pl.ds(pl.multiple_of(i * 128, 128), 128)
        x = tokens_ref[at, :].astype(jnp.float32)
        center = x - jnp.mean(x, axis=-1, keepdims=True)
        spread = jnp.mean(center * center, axis=-1, keepdims=True)
        h = center * lax.rsqrt(spread + EPSILON) * (1.0 + stretch) + offset
        hidden[:, at] = h.T.astype(jnp.bfloat16)
        return 0

    lax.fori_loop(0, T // 128, norm_rows, 0)

    def project(i, _):
        rows = weights_ref[pl.ds(i * group, group)].reshape(group * MAIN, D)
        out = jnp.dot(rows, hidden[...], preferred_element_type=jnp.float32)
        for j in range(group // 2):
            low = out[2 * j * MAIN : 2 * j * MAIN + QKV_ROWS]
            high = out[(2 * j + 1) * MAIN : (2 * j + 1) * MAIN + QKV_ROWS]
            both = jnp.concatenate([low, high], axis=0)
            for m in range(3):
                qkv[i * (3 * group // 2) + 3 * j + m] = both[m * HD : (m + 1) * HD].astype(jnp.bfloat16)
        for j in range(group):
            wo[pl.ds((i * group + j) * 48, 16), :] = weights_ref[i * group + j, 96:MAIN, :]
        return 0

    for i in range(SHARDS // group):
        loads[i].wait()
        project(i, 0)
        advance(2 if temporal else 1)

    def head_norm(values, column):
        values = values.astype(jnp.float32)
        square = jnp.mean(values * values, axis=0, keepdims=True)
        normed = values * lax.rsqrt(square + EPSILON) * gain[:, column : column + 1]
        if temporal:
            swapped = jnp.concatenate([normed[HD // 2 :], normed[: HD // 2]], axis=0)
            normed = normed * cos_ref[...] + swapped * sin_ref[...]
        return normed

    def head(h, _):
        q = head_norm(qkv[h], 0).astype(jnp.bfloat16)
        k = head_norm(qkv[HEADS + h], 1).T.astype(jnp.bfloat16)
        v = qkv[2 * HEADS + h]
        scores = jnp.dot(k, q, preferred_element_type=jnp.float32)
        exponent = jnp.exp2(scores * SCALE)
        if temporal:
            exponent = exponent * mask[...]
        total = jnp.sum(exponent, axis=0, keepdims=True)
        weights = (exponent * (1.0 / total)).astype(jnp.bfloat16)
        result = jnp.dot(v, weights, preferred_element_type=jnp.float32)
        attended[pl.ds(pl.multiple_of(h * HD, 8), HD), :] = result
        return 0

    for i in range(SEGMENTS):
        heads = HEADS // SEGMENTS
        lax.fori_loop(heads * i, heads * i + heads, head, 0, unroll=2)
        advance(PER_SEGMENT_T if temporal else PER_SEGMENT)
    if temporal:
        for _ in pump:
            pass
    else:
        rest_load.wait()
    attended_bf[...] = attended[...].astype(jnp.bfloat16)

    def output(i, _):
        for j in range(group):
            wo[pl.ds((i * group + j) * 48 + 16, REST), :] = rests_ref[i * group + j]
        rows = wo[pl.ds(i * 384, 384), :]
        out = jnp.dot(rows, attended_bf[...], preferred_element_type=jnp.float32)
        for j in range(4):
            both = jnp.concatenate([out[96 * j + 12 : 96 * j + 48], out[96 * j + 60 : 96 * j + 96]], axis=0)
            update[pl.ds((i * 4 + j) * 72, 72), :] = both
        return 0

    for i in range(4):
        output(i, 0)
        advance(1)

    def finish(i, _):
        at = pl.ds(pl.multiple_of(i * 128, 128), 128)
        value = tokens_ref[at, :].astype(jnp.float32) + gating * update[:, at].T
        if temporal:
            value = value * live_ref[at, :]
        out_ref[at, :] = value.astype(jnp.bfloat16)
        return 0

    lax.fori_loop(0, T // 128, finish, 0)
    for _ in pump:
        pass


GATHER_SCRATCH = [
    pltpu.SemaphoreType.DMA,
    pltpu.SemaphoreType.DMA((36,)),
    pltpu.SemaphoreType.DMA((36,)),
]


def block(tokens, weights, rest, mod, gain, shard=None, tables=()):
    temporal = shard is None
    vmem = pl.BlockSpec(memory_space=pltpu.VMEM)
    anywhere = pl.BlockSpec(memory_space=pl.ANY)
    operands = [tokens, weights, rest, mod, gain]
    specs = [vmem, anywhere, anywhere, vmem, vmem]
    out_shape = jax.ShapeDtypeStruct((T, D), jnp.bfloat16)
    out_specs = vmem
    scratch = [
        pltpu.VMEM((SHARDS, MAIN, D), jnp.bfloat16),
        pltpu.VMEM((SHARDS, REST, D), jnp.bfloat16),
        pltpu.SemaphoreType.DMA((5,)),
        *GATHER_SCRATCH,
        pltpu.VMEM((D, T), jnp.bfloat16),
        pltpu.VMEM((3 * HEADS, HD, T), jnp.bfloat16),
        pltpu.VMEM((D, T), jnp.float32),
        pltpu.VMEM((D, T), jnp.bfloat16),
        pltpu.VMEM((SHARDS * 48, D), jnp.bfloat16),
        pltpu.VMEM((D, T), jnp.float32),
    ]
    if temporal:
        operands += tables
        specs += [vmem] * 3
        scratch.append(pltpu.VMEM((T, T), jnp.float32))
    else:
        operands.append(shard)
        specs.append(anywhere)
        out_shape = (out_shape, jax.ShapeDtypeStruct((SHARDS, MAIN, D), jnp.bfloat16))
        out_specs = (out_specs, anywhere)
    return pl.pallas_call(
        functools.partial(block_kernel, temporal),
        out_shape=out_shape,
        in_specs=specs,
        out_specs=out_specs,
        scratch_shapes=scratch,
        compiler_params=pltpu.CompilerParams(
            vmem_limit_bytes=56 * 1024 * 1024,
            collective_id=2 if temporal else 1,
            has_side_effects=True,
        ),
        cost_estimate=pl.CostEstimate(flops=9 * 10**9, bytes_accessed=13 * 10**6, transcendentals=4 * 10**6),
    )(*operands)


def rotary_tables():
    frames = jnp.arange(T, dtype=jnp.float32) // 16.0
    frequency = jnp.power(10000.0, -2.0 * jnp.arange(HD // 2, dtype=jnp.float32) / HD)
    angles = frequency[:, None] * frames[None, :]
    cosine, sine = jnp.cos(angles), jnp.sin(angles)
    return jnp.concatenate([cosine, cosine], 0), jnp.concatenate([-sine, sine], 0)


MESH = pl.DeviceIdType.MESH


def seq_place():
    me = lax.axis_index("seq")
    core = lax.rem(me, 2)
    x, y = me // 8, lax.rem(me // 2, 4)
    first, second = jnp.where(core == 0, x, y), jnp.where(core == 0, y, x)
    first_stride, second_stride = jnp.where(core == 0, 8, 2), jnp.where(core == 0, 2, 8)
    return me, core, first, second, first_stride, second_stride


def seq_neighbours():
    me, core, first, second, first_stride, second_stride = seq_place()

    def at(da, db):
        return (
            lax.rem(first + da, 4) * first_stride + lax.rem(second + db, 4) * second_stride + core
        )

    return [{"seq": i} for i in (me + 1 - 2 * core, at(1, 0), at(3, 0), at(0, 1), at(0, 3))]


def greet(others):
    barrier = pltpu.get_barrier_semaphore()
    for other in others:
        pl.semaphore_signal(barrier, inc=1, device_id=other, device_id_type=MESH)
    pl.semaphore_wait(barrier, len(others))


def gather_steps(shard_ref, gathered_ref, own_sem, send_sem, recv_sem):
    me, core, first, second, first_stride, second_stride = seq_place()

    def at(da, db):
        return (
            lax.rem(first + da, 4) * first_stride + lax.rem(second + db, 4) * second_stride + core
        )

    sibling = me + 1 - 2 * core
    a_next, a_back, b_next, b_back = at(1, 0), at(3, 0), at(0, 1), at(0, 3)
    started = []
    count = shard_ref.shape[0]
    half = count // 32 * 16
    low, high, whole = pl.ds(0, half), pl.ds(half, count - half), pl.ds(0, count)

    def copy(kind, slot, rows, target, source=None):
        return pltpu.make_async_remote_copy(
            src_ref=gathered_ref.at[slot, rows] if source is None else source,
            dst_ref=gathered_ref.at[slot, rows],
            send_sem=send_sem.at[kind],
            recv_sem=recv_sem.at[kind],
            device_id={"seq": target},
            device_id_type=MESH,
        )

    def send(kind, slot, rows, target, source=None):
        made = copy(kind, slot, rows, target, source)
        made.start()
        started.append(made)

    def arrived(kind, slot, rows):
        copy(kind, slot, rows, sibling).wait_recv()

    def along_second(da, source=None):
        send(4 + 4 * da, at(da, 0), whole, b_next, source)
        send(5 + 4 * da, at(da, 0), whole, b_back, source)
        send(20 + 4 * da, at(da, 0), whole, sibling, source)

    def near(da):
        arrived(4 + 4 * da, at(da, 3), whole)
        send(6 + 4 * da, at(da, 3), low, b_next)
        send(20 + 4 * da + 3, at(da, 3), whole, sibling)
        yield
        arrived(5 + 4 * da, at(da, 1), whole)
        send(7 + 4 * da, at(da, 1), high, b_back)
        send(20 + 4 * da + 1, at(da, 1), whole, sibling)
        yield

    def far(da):
        arrived(6 + 4 * da, at(da, 2), low)
        arrived(7 + 4 * da, at(da, 2), high)
        send(20 + 4 * da + 2, at(da, 2), whole, sibling)
        yield

    send(0, me, whole, a_next, shard_ref)
    send(1, me, whole, a_back, shard_ref)
    along_second(0, shard_ref)
    own = pltpu.make_async_copy(shard_ref, gathered_ref.at[me], own_sem)
    own.start()
    yield
    arrived(0, at(3, 0), whole)
    send(2, at(3, 0), low, a_next)
    along_second(3)
    yield
    arrived(1, at(1, 0), whole)
    send(3, at(1, 0), high, a_back)
    along_second(1)
    yield
    yield from near(0)
    arrived(2, at(2, 0), low)
    arrived(3, at(2, 0), high)
    along_second(2)
    yield
    yield from near(3)
    yield from near(1)
    yield from far(0)
    yield from near(2)
    yield from far(3)
    yield from far(1)
    yield from far(2)
    for da in range(4):
        for db in range(4):
            mine = (
                lax.rem(second + da, 4) * second_stride
                + lax.rem(first + db, 4) * first_stride
                + 1
                - core
            )
            arrived(20 + 4 * da + db, mine, whole)
    for made in started:
        made.wait_send()
    own.wait()


def first_kernel(shard_ref, rest_ref, outgoing_ref, gathered_ref, rests_ref, tokens_ref,
                 own_sem, send_sem, recv_sem, rest_own_sem, rest_send_sem, rest_recv_sem,
                 keep_sem, out_sem, in_sem):
    here = lax.axis_index("group")
    clips = outgoing_ref.shape[0]
    peers = [lax.rem(here + d, clips) for d in range(1, clips)]
    greet(seq_neighbours() + [{"group": peer} for peer in peers])
    keep = pltpu.make_async_copy(outgoing_ref.at[here], tokens_ref.at[here], keep_sem)
    keep.start()
    sent = []
    for d in range(1, clips):
        sent.append(
            pltpu.make_async_remote_copy(
                src_ref=outgoing_ref.at[peers[d - 1]],
                dst_ref=tokens_ref.at[here],
                send_sem=out_sem.at[d - 1],
                recv_sem=in_sem.at[d - 1],
                device_id={"group": peers[d - 1]},
                device_id_type=MESH,
            )
        )
        sent[-1].start()
    main = gather_steps(shard_ref, gathered_ref, own_sem, send_sem, recv_sem)
    next(main)
    rest = gather_steps(rest_ref, rests_ref, rest_own_sem, rest_send_sem, rest_recv_sem)
    next(rest)
    for _ in main:
        next(rest, None)
    for _ in rest:
        pass
    for made in sent:
        made.wait()
    keep.wait()


def first_exchange(rows, rest, outgoing):
    anywhere = pl.BlockSpec(memory_space=pl.ANY)
    clips = outgoing.shape[0]
    return pl.pallas_call(
        first_kernel,
        out_shape=(
            jax.ShapeDtypeStruct((SHARDS, MAIN, D), jnp.bfloat16),
            jax.ShapeDtypeStruct((SHARDS, REST, D), jnp.bfloat16),
            jax.ShapeDtypeStruct(outgoing.shape, outgoing.dtype),
        ),
        in_specs=[anywhere] * 3,
        out_specs=(anywhere,) * 3,
        scratch_shapes=GATHER_SCRATCH * 2
        + [
            pltpu.SemaphoreType.DMA,
            pltpu.SemaphoreType.DMA((clips - 1,)),
            pltpu.SemaphoreType.DMA((clips - 1,)),
        ],
        compiler_params=pltpu.CompilerParams(collective_id=0, has_side_effects=True),
        cost_estimate=pl.CostEstimate(flops=0, bytes_accessed=60 * 10**6, transcendentals=0),
    )(rows, rest, outgoing)


def shard_rows(project, output):
    return jnp.concatenate([project.T, output.T], axis=0)


def on_device(
    latents,
    sampler_order,
    frame_counts,
    modulation,
    spatial_project,
    spatial_output,
    spatial_gain,
    temporal_project,
    temporal_output,
    temporal_gain,
):
    clip_id = sampler_order[lax.axis_index("group")]
    length = frame_counts[clip_id]
    mod = lax.dynamic_index_in_dim(modulation, clip_id, 0, keepdims=False)
    outgoing = latents.at[sampler_order].get(mode="promise_in_bounds")
    spatial_rows = shard_rows(spatial_project, spatial_output)
    temporal_rows = shard_rows(temporal_project, temporal_output)
    spatial_weights, spatial_rest, arrived = first_exchange(
        spatial_rows[:MAIN], spatial_rows[MAIN:], outgoing.reshape(-1, latents.shape[2], D)
    )
    mixture, temporal_weights = block(
        arrived.reshape(T, D),
        spatial_weights,
        spatial_rest,
        mod,
        spatial_gain,
        shard=temporal_rows[:MAIN],
    )
    by_position = lax.all_to_all(
        mixture.reshape(SHARDS, T // SHARDS, D), "seq", split_axis=0, concat_axis=0, tiled=True
    )
    live = (jnp.arange(T, dtype=jnp.int32)[:, None] // 16 < length).astype(jnp.float32)
    finished = block(
        by_position.reshape(T, D),
        temporal_weights,
        temporal_rows[MAIN:],
        mod,
        temporal_gain,
        tables=(live, *rotary_tables()),
    )
    returned = lax.all_to_all(
        finished.reshape(SHARDS, T // SHARDS, D), "seq", split_axis=0, concat_axis=0, tiled=True
    )
    return returned.reshape(1, 1, T, D)


def solution(mesh):
    in_specs = (
        P(None, "seq", "group", None),
        P(),
        P(),
        P(),
        P(None, "seq"),
        P(None, "seq"),
        P(),
        P(None, "seq"),
        P(None, "seq"),
        P(),
    )
    out_specs = P("group", "seq", None, None)
    return jax.shard_map(
        on_device, mesh=mesh, in_specs=in_specs, out_specs=out_specs, check_vma=False
    )
```
